32 devices in a mesh: groups: 2 (over y), ctx: 4 (over z), heads: 2 (over x), sub: 2 (over core).
Axes of the slice: x: 2, y: 2, z: 4, core: 2. Of those that a mesh axis runs over, the one named last changes fastest.
Arguments:
- queries: bfloat16 [2048, 4096], P(('groups', 'ctx', 'sub'), 'heads'), parts along dimension 0, may hold values from -6 to 6
- keys: bfloat16 [2048, 1024], P(('groups', 'ctx'), 'heads'), parts along dimension 0, may hold values from -6 to 6
- values: bfloat16 [2048, 1024], P(('groups', 'ctx'), 'heads'), parts along dimension 0, may hold values from -6 to 6
- image_keys: bfloat16 [256, 1024], P(('groups', 'ctx', 'sub'), 'heads'), parts along dimension 0, may hold values from -6 to 6
- image_values: bfloat16 [256, 1024], P(('groups', 'ctx', 'sub'), 'heads'), parts along dimension 0, may hold values from -6 to 6
- image_lengths: int32 [16], P('groups'), parts along dimension 0, may hold values from 1 to 32, 128 in all
- token_images: int32 [2048], P('groups'), parts along dimension 0, may hold values from 0 to 8, as said below
Outputs:
- self_out: bfloat16 [2048, 4096], P(('groups', 'ctx', 'sub'), 'heads'), parts along dimension 0
- cross_out: bfloat16 [2048, 4096], P(('groups', 'ctx', 'sub'), 'heads'), parts along dimension 0
The draws below stay inside these ranges and needn't reach their ends.
There are 2 independent parts, one for each index of `groups`. The reference program is written for one: setup_inputs(seed, part) draws one part's arguments, and reference() takes and returns one part's arrays. A program takes and returns all parts, laid end to end along the dimension named above; each array names one. Nothing has to cross between parts.
Inputs may be any that keep to these rules, and one draw needn't show every extreme that they name: `token_images`: never falls along the sequence; the first token sees no image and the last sees all 8.
All inputs are finite; a program needn't handle non-finite values.
Results may differ from the reference program's by a relative error of at most 0.005.
Values may be sent and summed in bfloat16 or wider, within the bound.
A program may use at most 128 MiB of HBM per device.

```python
import math
import jax
import jax.numpy as jnp
import numpy as np
from jax import lax

QH = 32
KVH = 8
HD = 128
NIMG = 8
LEN = 1024
NV = 128


def draw_queries(key, part):
    shape = (LEN, QH * HD)
    return jnp.clip(jax.random.normal(jax.random.fold_in(key, 1), shape, jnp.float32), -6.0, 6.0).astype(jnp.bfloat16)


def draw_keys(key, part):
    shape = (LEN, KVH * HD)
    return jnp.clip(jax.random.normal(jax.random.fold_in(key, 2), shape, jnp.float32), -6.0, 6.0).astype(jnp.bfloat16)


def draw_image_keys(key, part):
    shape = (NV, KVH * HD)
    return jnp.clip(jax.random.normal(jax.random.fold_in(key, 3), shape, jnp.float32), -6.0, 6.0).astype(jnp.bfloat16)


def draw_token_images(key, part):
    spacing = LEN // NIMG
    jitter = jax.random.randint(jax.random.fold_in(key, 4), (NIMG,), 0, LEN // (2 * NIMG))
    first_token = 1 + jnp.arange(NIMG, dtype=jnp.int32) * spacing + jitter
    tokens_here = jnp.arange(LEN, dtype=jnp.int32)
    return jnp.sum((tokens_here[:, None] >= first_token[None, :]).astype(jnp.int32), axis=1).astype(jnp.int32)


def shard_levels(stream_key, dims, cuts, least, high):
    level = 1.0
    for axis_at, blocks in cuts:
        draws = jax.random.uniform(jax.random.fold_in(jax.random.fold_in(stream_key, 6), axis_at), (blocks,), jnp.float32, least / len(cuts), high / len(cuts))
        level = level * jnp.repeat(jnp.exp(draws), dims[axis_at] // blocks).reshape((-1,) + (1,) * (len(dims) - 1 - axis_at))
    return level


def split_up(count, total, limit, lean):
    portions = [(1 << 20) // math.isqrt(standing ** lean) + 1 for standing in range(2, count + 1)]
    surplus, holding = total - limit - (count - 1), [1] * (count - 1)
    while surplus > 0:
        candidates = [i for i in range(count - 1) if holding[i] < limit]
        whole, left = sum([portions[i] for i in candidates]), surplus
        for i in candidates:
            extra = min(limit - holding[i], max(1, left * portions[i] // whole), surplus)
            holding[i] = holding[i] + extra
            surplus = surplus - extra
    return np.array([limit] + holding)


def uneven_parts(stream_key, count, total, limit, slope):
    if count == 2:
        one = jax.random.randint(stream_key, (), max(1, total - limit), min(limit, total - 1) + 1)
        return jnp.stack([one, total - one])
    sizes = jnp.asarray(split_up(count, total, limit, slope), jnp.int32)
    pairs = (count - 1) // 2
    donor, receiver = sizes[1:1 + 2 * pairs:2], sizes[2:2 + 2 * pairs:2]
    room = jnp.minimum(donor - 1, limit - receiver)
    moved = jax.random.randint(jax.random.fold_in(stream_key, 1), (pairs,), 0, 1 << 20) % (room + 1)
    sizes = sizes.at[1:1 + 2 * pairs:2].set(donor - moved).at[2:2 + 2 * pairs:2].set(receiver + moved)
    return sizes[jax.random.permutation(jax.random.fold_in(stream_key, 2), count)]


def gaussian(rng, dims, scale, bound, split=(), held_as=jnp.bfloat16):
    factor_of = shard_levels(rng, dims, split, -0.22, 0.18) if split else 1.0
    entries = jax.random.normal(rng, dims, jnp.float32) * scale * factor_of
    return jnp.minimum(jnp.maximum(entries, -bound), bound).astype(held_as)


def setup_inputs(seed: int = 0, part: int = 0) -> dict:
    seeds = jax.random.split(jax.random.key(seed), 8)
    part_keys = jax.random.split(jax.random.fold_in(seeds[7], part), 8)
    queries = draw_queries(jax.random.fold_in(jax.random.fold_in(seeds[7], part), 71), part)
    keys = draw_keys(jax.random.fold_in(jax.random.fold_in(seeds[7], part), 71), part)
    values = gaussian(part_keys[2], (LEN, KVH * HD), 1.0, 6.0, ((0, 4), (1, 2)))
    image_keys = draw_image_keys(jax.random.fold_in(jax.random.fold_in(seeds[7], part), 71), part)
    image_values = gaussian(part_keys[4], (NV, KVH * HD), 1.0, 6.0, ((0, 8), (1, 2)))
    image_lengths = uneven_parts(part_keys[5], NIMG, NV, NV // 4, 2).astype(jnp.int32)
    token_images = draw_token_images(jax.random.fold_in(jax.random.fold_in(seeds[7], part), 71), part)
    return {"queries": queries, "keys": keys, "values": values, "image_keys": image_keys, "image_values": image_values, "image_lengths": image_lengths, "token_images": token_images}


def attend_heads(queries, keys, values, allowed, has_image):
    score_scale = 1.0 / math.sqrt(HD)
    group_size = QH // KVH

    def one_head(head):
        query_cols = lax.dynamic_slice_in_dim(queries, head * HD, HD, 1)
        key_cols = lax.dynamic_slice_in_dim(keys, head // group_size * HD, HD, 1)
        value_cols = lax.dynamic_slice_in_dim(values, head // group_size * HD, HD, 1)
        scores = jnp.dot(query_cols, key_cols.T, preferred_element_type=jnp.float32) * score_scale
        scores = jnp.where(allowed, scores, -1e+30)
        row_max = lax.optimization_barrier(jnp.max(scores, axis=1, keepdims=True))
        weights = jnp.where(allowed, jnp.exp(scores - row_max), 0.0)
        row_sum = lax.optimization_barrier(jnp.sum(weights, axis=1))
        result = jnp.dot(weights.astype(jnp.bfloat16), value_cols, preferred_element_type=jnp.float32)
        safe_sum = jnp.where(has_image, row_sum, 1.0)
        result = jnp.where(has_image[:, None], result / safe_sum[:, None], 0.0)
        return result.astype(jnp.bfloat16)
    stacked = lax.map(one_head, jnp.arange(QH, dtype=jnp.int32))
    return stacked.transpose(1, 0, 2).reshape(queries.shape[0], QH * HD)

def reference(queries, keys, values, image_keys, image_values, image_lengths, token_images):
    positions = jnp.arange(LEN, dtype=jnp.int32)
    causal = positions[None, :] <= positions[:, None]
    everyone = jnp.ones((LEN,), dtype=bool)
    self_out = attend_heads(queries, keys, values, causal, everyone)
    image_index = jnp.arange(NIMG, dtype=jnp.int32)
    visible = lax.optimization_barrier(jnp.sum(jnp.where(image_index[None, :] < token_images[:, None], image_lengths[None, :], 0), axis=1)).astype(jnp.int32)
    image_pos = jnp.arange(NV, dtype=jnp.int32)
    seen = image_pos[None, :] < visible[:, None]
    cross_out = attend_heads(queries, image_keys, image_values, seen, visible > 0)
    return (self_out, cross_out)
```

```python
import functools
import math

import jax
import jax.numpy as jnp
from jax import lax
from jax.experimental import pallas as pl
from jax.experimental.pallas import tpu as pltpu
from jax.sharding import PartitionSpec as P

HD = 128
MESH = pl.DeviceIdType.MESH
LOW = -1e30
SCALE = math.log2(math.e) / math.sqrt(HD)


def kernel(
    n, subs, lengths, tokens, q_hbm, k_hbm, v_hbm, ik_hbm, iv_hbm, self_ref, cross_ref,
    q, k, v, qt, kv, img, run_max, run_sum, run_out,
    in_sem, text_recv, up_send, side_send, img_recv, img_send, img_side,
):
    c, s = lax.axis_index("ctx"), lax.axis_index("sub")
    rows, span = q.shape[0], k.shape[0]
    heads = k.shape[1] // HD
    share = heads // subs
    group = q.shape[1] // k.shape[1]
    image_rows = img.shape[2]
    mine = c * subs + s

    def sibling(d):
        return {"sub": lax.rem(s + d, subs)}

    loads = [
        pltpu.make_async_copy(src, dst, in_sem.at[i])
        for i, (src, dst) in enumerate(
            [(k_hbm, k), (v_hbm, v), (ik_hbm, img.at[mine, 0]), (iv_hbm, img.at[mine, 1]), (q_hbm, q)]
        )
    ]
    for load in loads:
        load.start()

    barrier = pltpu.get_barrier_semaphore()

    @pl.loop(1, n)
    def _(d):
        pl.semaphore_signal(barrier, inc=1, device_id={"ctx": lax.rem(c + d, n)}, device_id_type=MESH)

    for d in range(1, subs):
        pl.semaphore_signal(barrier, inc=1, device_id=sibling(d), device_id_type=MESH)

    loads[0].wait()
    for j in range(heads):
        kv[c, j, 0] = k[:, j * HD:(j + 1) * HD]
    loads[1].wait()
    for j in range(heads):
        for i in range(span // HD):
            kv[c, j, 1, i * HD:(i + 1) * HD] = v[i * HD:(i + 1) * HD, j * HD:(j + 1) * HD].T
    loads[2].wait()
    loads[3].wait()
    pl.semaphore_wait(barrier, n - 1 + subs - 1)

    def up(b, i):
        j = s * share + i
        return pltpu.make_async_remote_copy(
            kv.at[b, j], kv.at[b, j], up_send.at[b, i], text_recv.at[b, j],
            device_id={"ctx": lax.rem(c + 1, n)}, device_id_type=MESH,
        )

    def side(b, j, i, d):
        return pltpu.make_async_remote_copy(
            kv.at[b, j], kv.at[b, j], side_send.at[b, i, d - 1], text_recv.at[b, j],
            device_id=sibling(d), device_id_type=MESH,
        )

    def image_to(d):
        return pltpu.make_async_remote_copy(
            img.at[mine], img.at[mine], img_send.at[d - 1], img_recv.at[mine],
            device_id={"ctx": lax.rem(c + d, n)}, device_id_type=MESH,
        )

    def image_side(cc, ss, d):
        at = cc * subs + ss
        return pltpu.make_async_remote_copy(
            img.at[at], img.at[at], img_side.at[cc, d - 1], img_recv.at[at],
            device_id=sibling(d), device_id_type=MESH,
        )

    @pl.loop(1, n)
    def _(d):
        image_to(d).start()

    for d in range(1, subs):
        image_side(c, s, d).start()

    @pl.when(c < n - 1)
    def _():
        for i in range(share):
            up(c, i).start()

    loads[4].wait()
    for j in range(heads):
        for g in range(group):
            h = j * group + g
            qt[j, :, g * rows:(g + 1) * rows] = q[:, h * HD:(h + 1) * HD].T

    def scores(j, key_rows):
        return jnp.dot(key_rows, qt[j], preferred_element_type=jnp.float32) * SCALE

    def wide(x):
        return jnp.concatenate([x] * group, axis=1)

    def put(ref, j, out):
        out = out.astype(jnp.bfloat16)
        for g in range(group):
            at = pl.multiple_of((j * group + g) * HD, HD)
            ref[:, pl.ds(at, HD)] = out[:, g * rows:(g + 1) * rows].T

    def values_of(b, j):
        return jnp.concatenate([kv[b, j, 1, i * HD:(i + 1) * HD] for i in range(span // HD)], axis=1)

    def finish(j):
        put(self_ref, j, run_out[j] * (1.0 / run_sum[j]))

    key_at = lax.broadcasted_iota(jnp.int32, (span, rows), 0)
    row_at = lax.broadcasted_iota(jnp.int32, (span, rows), 1) + s * rows
    bias = wide(jnp.where(key_at <= row_at, 0.0, LOW))
    for j in range(heads):
        sc = scores(j, kv[c, j, 0]) + bias
        top = jnp.max(sc, axis=0, keepdims=True)
        w = jnp.exp2(sc - top)
        run_max[j] = top
        run_sum[j] = jnp.sum(w, axis=0, keepdims=True)
        run_out[j] = jnp.dot(values_of(c, j), w.astype(jnp.bfloat16), preferred_element_type=jnp.float32)

    @pl.when(c == 0)
    def _():
        for j in range(heads):
            finish(j)

    @pl.loop(1, n)
    def _(d):
        cc = lax.rem(c + d, n)
        image_side(cc, s, 1).wait_recv()
        for e in range(1, subs):
            image_side(cc, s, e).start()

    @pl.loop(0, n)
    def _(cc):
        for e in range(1, subs):
            image_side(cc, lax.rem(s + e, subs), e).wait_recv()

    seen_images = tokens[pl.ds(mine, 1), :]
    visible = jnp.zeros_like(seen_images)
    for i in range(lengths.shape[0]):
        visible = visible + jnp.where(seen_images > i, lengths[i], 0)
    visible = wide(visible)
    count = n * subs * image_rows
    allowed = lax.broadcasted_iota(jnp.int32, (count, group * rows), 0) < visible
    for j in range(heads):
        cols = slice(j * HD, (j + 1) * HD)
        sc = jnp.where(allowed, scores(j, img[:, 0, :, cols].reshape(count, HD)), LOW)
        top = jnp.max(sc, axis=0, keepdims=True)
        w = jnp.where(allowed, jnp.exp2(sc - top), 0.0)
        total = jnp.sum(w, axis=0, keepdims=True)
        out = jnp.dot(
            img[:, 1, :, cols].reshape(count, HD).T, w.astype(jnp.bfloat16),
            preferred_element_type=jnp.float32,
        )
        out = jnp.where(visible > 0, out * (1.0 / jnp.where(visible > 0, total, 1.0)), 0.0)
        put(cross_ref, j, out)

    def attend(b, j):
        sc = scores(j, kv[b, j, 0])
        old = run_max[j]
        top = jnp.maximum(old, jnp.max(sc, axis=0, keepdims=True))
        w = jnp.exp2(sc - top)
        factor = jnp.exp2(old - top)
        run_max[j] = top
        run_sum[j] = run_sum[j] * factor + jnp.sum(w, axis=0, keepdims=True)
        run_out[j] = run_out[j] * factor + jnp.dot(
            values_of(b, j), w.astype(jnp.bfloat16), preferred_element_type=jnp.float32
        )

        @pl.when(b == 0)
        def _():
            finish(j)

    @pl.loop(1, c + 1)
    def _(t):
        b = c - t
        for i in range(share):
            up(b, i).wait_recv()

            @pl.when(c < n - 1)
            def _():
                up(b, i).start()

            for d in range(1, subs):
                side(b, s * share + i, i, d).start()
            attend(b, s * share + i)
            for d in range(1, subs):
                j = lax.rem(s + d, subs) * share + i
                side(b, j, i, d).wait_recv()
                attend(b, j)

    @pl.loop(1, n)
    def _(d):
        image_to(d).wait_send()

    @pl.loop(0, n)
    def _(cc):
        for d in range(1, subs):
            image_side(cc, s, d).wait_send()

    @pl.when(c < n - 1)
    def _():
        @pl.loop(0, c + 1)
        def _(b):
            for i in range(share):
                up(b, i).wait_send()

    @pl.loop(0, c)
    def _(b):
        for i in range(share):
            for d in range(1, subs):
                side(b, s * share + i, i, d).wait_send()


def local(queries, keys, values, image_keys, image_values, image_lengths, token_images):
    n, subs = lax.axis_size("ctx"), lax.axis_size("sub")
    rows, wide = queries.shape
    span, narrow = keys.shape
    heads, image_rows = narrow // HD, image_keys.shape[0]
    group = wide // narrow
    share = heads // subs
    vmem = pl.BlockSpec(memory_space=pltpu.VMEM)
    hbm = pl.BlockSpec(memory_space=pl.ANY)
    dma = pltpu.SemaphoreType.DMA
    out = jax.ShapeDtypeStruct((rows, wide), jnp.bfloat16)
    return pl.pallas_call(
        functools.partial(kernel, n, subs),
        out_shape=(out, out),
        in_specs=[pl.BlockSpec(memory_space=pltpu.SMEM), vmem, hbm, hbm, hbm, hbm, hbm],
        out_specs=(vmem, vmem),
        scratch_shapes=[
            pltpu.VMEM((rows, wide), jnp.bfloat16),
            pltpu.VMEM((span, narrow), jnp.bfloat16),
            pltpu.VMEM((span, narrow), jnp.bfloat16),
            pltpu.VMEM((heads, HD, group * rows), jnp.bfloat16),
            pltpu.VMEM((n, heads, 2, span, HD), jnp.bfloat16),
            pltpu.VMEM((n * subs, 2, image_rows, narrow), jnp.bfloat16),
            pltpu.VMEM((heads, 1, group * rows), jnp.float32),
            pltpu.VMEM((heads, 1, group * rows), jnp.float32),
            pltpu.VMEM((heads, HD, group * rows), jnp.float32),
            dma((5,)),
            dma((n, heads)),
            dma((n, share)),
            dma((n, share, subs - 1)),
            dma((n * subs,)),
            dma((n - 1,)),
            dma((n, subs - 1)),
        ],
        compiler_params=pltpu.CompilerParams(
            collective_id=0, has_side_effects=True, vmem_limit_bytes=40 * 1024 * 1024
        ),
    )(image_lengths, token_images.reshape(-1, rows), queries, keys, values, image_keys, image_values)


def solution(mesh):
    fine = P(("groups", "ctx", "sub"), "heads")
    block = P(("groups", "ctx"), "heads")
    in_specs = (fine, block, block, fine, fine, P("groups"), P("groups"))
    return jax.shard_map(local, mesh=mesh, in_specs=in_specs, out_specs=(fine, fine), check_vma=False)
```

```python
import functools
import math

import jax
import jax.numpy as jnp
from jax import lax
from jax.experimental import pallas as pl
from jax.experimental.pallas import tpu as pltpu
from jax.sharding import PartitionSpec as P

HD = 128
MESH = pl.DeviceIdType.MESH
LOW = -1e30
SCALE = math.log2(math.e) / math.sqrt(HD)


def kernel(
    n, subs, len_hbm, tok_hbm, q_hbm, k_hbm, v_hbm, ik_hbm, iv_hbm, self_ref, cross_ref,
    lengths, tokens, q, k, v, qt, kv, img, run_max, run_sum, run_out,
    in_sem, text_recv, up_send, side_send, img_recv, img_send, img_side,
):
    c, s = lax.axis_index("ctx"), lax.axis_index("sub")
    rows, span = q.shape[0], k.shape[0]
    heads = k.shape[1] // HD
    part = span // subs
    group = q.shape[1] // k.shape[1]
    image_rows = img.shape[2]
    mine = c * subs + s

    def sibling(d):
        return {"sub": lax.rem(s + d, subs)}

    barrier = pltpu.get_barrier_semaphore()

    @pl.loop(1, n)
    def _(d):
        pl.semaphore_signal(barrier, inc=1, device_id={"ctx": lax.rem(c + d, n)}, device_id_type=MESH)

    for d in range(1, subs):
        pl.semaphore_signal(barrier, inc=1, device_id=sibling(d), device_id_type=MESH)

    loads = [
        pltpu.make_async_copy(src, dst, in_sem.at[i])
        for i, (src, dst) in enumerate(
            [
                (k_hbm, k), (v_hbm, v), (ik_hbm, img.at[mine, 0]), (iv_hbm, img.at[mine, 1]),
                (q_hbm, q), (len_hbm, lengths), (tok_hbm, tokens),
            ]
        )
    ]
    for load in loads:
        load.start()

    def lay_out(ss):
        for j in range(heads):
            cols = slice(j * HD, (j + 1) * HD)
            kv[c, j, ss, 0] = k[pl.ds(ss * part, part), cols]
            for i in range(0, part, HD):
                kv[c, j, ss, 1, i:i + HD] = v[pl.ds(ss * part + i, HD), cols].T

    loads[0].wait()
    loads[1].wait()
    lay_out(s)
    loads[2].wait()
    loads[3].wait()
    pl.semaphore_wait(barrier, n - 1 + subs - 1)

    def up(b, j):
        return pltpu.make_async_remote_copy(
            kv.at[b, j, s], kv.at[b, j, s], up_send.at[b, j], text_recv.at[b, j, s],
            device_id={"ctx": lax.rem(c + 1, n)}, device_id_type=MESH,
        )

    def side(b, j, ss, d):
        return pltpu.make_async_remote_copy(
            kv.at[b, j, ss], kv.at[b, j, ss], side_send.at[b, j, d - 1], text_recv.at[b, j, ss],
            device_id=sibling(d), device_id_type=MESH,
        )

    def image_to(d):
        return pltpu.make_async_remote_copy(
            img.at[mine], img.at[mine], img_send.at[d - 1], img_recv.at[mine],
            device_id={"ctx": lax.rem(c + d, n)}, device_id_type=MESH,
        )

    def image_side(cc, ss, d):
        at = cc * subs + ss
        return pltpu.make_async_remote_copy(
            img.at[at], img.at[at], img_side.at[cc, d - 1], img_recv.at[at],
            device_id=sibling(d), device_id_type=MESH,
        )

    @pl.loop(1, n)
    def _(d):
        image_to(d).start()

    for d in range(1, subs):
        image_side(c, s, d).start()

    @pl.when(c < n - 1)
    def _():
        for j in range(heads):
            up(c, j).start()

    for d in range(1, subs):
        lay_out(lax.rem(s + d, subs))
    loads[4].wait()
    for j in range(heads):
        for g in range(group):
            h = j * group + g
            qt[j, :, g * rows:(g + 1) * rows] = q[:, h * HD:(h + 1) * HD].T

    def scores(j, key_rows):
        return jnp.dot(key_rows, qt[j], preferred_element_type=jnp.float32) * SCALE

    def wide(x):
        return jnp.concatenate([x] * group, axis=1)

    def put(ref, j, out):
        out = out.astype(jnp.bfloat16)
        for g in range(group):
            at = (j * group + g) * HD
            if not isinstance(at, int):
                at = pl.multiple_of(at, HD)
            ref[:, pl.ds(at, HD)] = out[:, g * rows:(g + 1) * rows].T

    def keys_of(b, j):
        return jnp.concatenate([kv[b, j, ss, 0] for ss in range(subs)], axis=0)

    def values_of(b, j):
        return jnp.concatenate(
            [kv[b, j, ss, 1, i:i + HD] for ss in range(subs) for i in range(0, part, HD)], axis=1
        )

    def finish(j):
        put(self_ref, j, run_out[j] * (1.0 / run_sum[j]))

    key_at = lax.broadcasted_iota(jnp.int32, (span, rows), 0)
    row_at = lax.broadcasted_iota(jnp.int32, (span, rows), 1) + s * rows
    bias = wide(jnp.where(key_at <= row_at, 0.0, LOW))
    for j in range(heads):
        sc = scores(j, keys_of(c, j)) + bias
        top = jnp.max(sc, axis=0, keepdims=True)
        w = jnp.exp2(sc - top)
        run_max[j] = top
        run_sum[j] = jnp.sum(w, axis=0, keepdims=True)
        run_out[j] = jnp.dot(values_of(c, j), w.astype(jnp.bfloat16), preferred_element_type=jnp.float32)

    @pl.when(c == 0)
    def _():
        for j in range(heads):
            finish(j)

    @pl.loop(1, n)
    def _(d):
        cc = lax.rem(c + d, n)
        image_side(cc, s, 1).wait_recv()
        for e in range(1, subs):
            image_side(cc, s, e).start()

    @pl.loop(0, n)
    def _(cc):
        for e in range(1, subs):
            image_side(cc, lax.rem(s + e, subs), e).wait_recv()

    loads[5].wait()
    loads[6].wait()
    seen_images = tokens[pl.ds(mine, 1), :]
    visible = jnp.zeros_like(seen_images)
    for i in range(lengths.shape[0]):
        visible = visible + jnp.where(seen_images > i, lengths[i], 0)
    visible = wide(visible)
    count = n * subs * image_rows
    allowed = lax.broadcasted_iota(jnp.int32, (count, group * rows), 0) < visible
    for j in range(heads):
        cols = slice(j * HD, (j + 1) * HD)
        sc = jnp.where(allowed, scores(j, img[:, 0, :, cols].reshape(count, HD)), LOW)
        top = jnp.max(sc, axis=0, keepdims=True)
        w = jnp.where(allowed, jnp.exp2(sc - top), 0.0)
        total = jnp.sum(w, axis=0, keepdims=True)
        out = jnp.dot(
            img[:, 1, :, cols].reshape(count, HD).T, w.astype(jnp.bfloat16),
            preferred_element_type=jnp.float32,
        )
        out = jnp.where(visible > 0, out * (1.0 / jnp.where(visible > 0, total, 1.0)), 0.0)
        put(cross_ref, j, out)

    def attend(b, j):
        sc = scores(j, keys_of(b, j))
        old = run_max[j]
        top = jnp.maximum(old, jnp.max(sc, axis=0, keepdims=True))
        w = jnp.exp2(sc - top)
        factor = jnp.exp2(old - top)
        run_max[j] = top
        run_sum[j] = run_sum[j] * factor + jnp.sum(w, axis=0, keepdims=True)
        run_out[j] = run_out[j] * factor + jnp.dot(
            values_of(b, j), w.astype(jnp.bfloat16), preferred_element_type=jnp.float32
        )

        @pl.when(b == 0)
        def _():
            finish(j)

    def place(x):
        return c - 1 - lax.div(x, heads), lax.rem(x, heads)

    @pl.loop(0, c * heads + jnp.where(c > 0, 1, 0))
    def _(x):
        @pl.when(x < c * heads)
        def _():
            b, j = place(x)
            up(b, j).wait_recv()

            @pl.when(c < n - 1)
            def _():
                up(b, j).start()

            for d in range(1, subs):
                side(b, j, s, d).start()

        @pl.when(x > 0)
        def _():
            b, j = place(x - 1)
            for d in range(1, subs):
                side(b, j, lax.rem(s + d, subs), d).wait_recv()
            attend(b, j)

    @pl.loop(1, n)
    def _(d):
        image_to(d).wait_send()

    @pl.loop(0, n)
    def _(cc):
        for d in range(1, subs):
            image_side(cc, s, d).wait_send()

    @pl.when(c < n - 1)
    def _():
        @pl.loop(0, c + 1)
        def _(b):
            for j in range(heads):
                up(b, j).wait_send()

    @pl.loop(0, c)
    def _(b):
        for j in range(heads):
            for d in range(1, subs):
                side(b, j, s, d).wait_send()


def local(queries, keys, values, image_keys, image_values, image_lengths, token_images):
    n, subs = lax.axis_size("ctx"), lax.axis_size("sub")
    rows, wide = queries.shape
    span, narrow = keys.shape
    heads, image_rows = narrow // HD, image_keys.shape[0]
    group = wide // narrow
    vmem = pl.BlockSpec(memory_space=pltpu.VMEM)
    hbm = pl.BlockSpec(memory_space=pl.ANY)
    dma = pltpu.SemaphoreType.DMA
    out = jax.ShapeDtypeStruct((rows, wide), jnp.bfloat16)
    token_images = token_images.reshape(-1, rows)
    return pl.pallas_call(
        functools.partial(kernel, n, subs),
        out_shape=(out, out),
        in_specs=[hbm] * 7,
        out_specs=(vmem, vmem),
        scratch_shapes=[
            pltpu.SMEM(image_lengths.shape, jnp.int32),
            pltpu.VMEM(token_images.shape, jnp.int32),
            pltpu.VMEM((rows, wide), jnp.bfloat16),
            pltpu.VMEM((span, narrow), jnp.bfloat16),
            pltpu.VMEM((span, narrow), jnp.bfloat16),
            pltpu.VMEM((heads, HD, group * rows), jnp.bfloat16),
            pltpu.VMEM((n, heads, subs, 2, span // subs, HD), jnp.bfloat16),
            pltpu.VMEM((n * subs, 2, image_rows, narrow), jnp.bfloat16),
            pltpu.VMEM((heads, 1, group * rows), jnp.float32),
            pltpu.VMEM((heads, 1, group * rows), jnp.float32),
            pltpu.VMEM((heads, HD, group * rows), jnp.float32),
            dma((7,)),
            dma((n, heads, subs)),
            dma((n, heads)),
            dma((n, heads, subs - 1)),
            dma((n * subs,)),
            dma((n - 1,)),
            dma((n, subs - 1)),
        ],
        compiler_params=pltpu.CompilerParams(
            collective_id=0, has_side_effects=True, vmem_limit_bytes=62 * 1024 * 1024
        ),
    )(image_lengths, token_images, queries, keys, values, image_keys, image_values)


def solution(mesh):
    fine = P(("groups", "ctx", "sub"), "heads")
    block = P(("groups", "ctx"), "heads")
    in_specs = (fine, block, block, fine, fine, P("groups"), P("groups"))
    return jax.shard_map(local, mesh=mesh, in_specs=in_specs, out_specs=(fine, fine), check_vma=False)
```

```python
import functools
import math

import jax
import jax.numpy as jnp
from jax import lax
from jax.experimental import pallas as pl
from jax.experimental.pallas import tpu as pltpu
from jax.sharding import PartitionSpec as P

HD = 128
MESH = pl.DeviceIdType.MESH
LOW = -1e30
SCALE = math.log2(math.e) / math.sqrt(HD)


def kernel(
    n, subs, len_hbm, tok_hbm, q_hbm, k_hbm, v_hbm, ik_hbm, iv_hbm, self_ref, cross_ref,
    lengths, tokens, q, k, v, qt, kv, img, run_max, run_sum, run_out,
    guest_q, guest_max, guest_sum, guest_out, part_out, part_stats,
    in_sem, text_recv, up_send, side_send, img_recv, img_up, img_down, img_side,
    q_send, q_recv, part_send, part_recv,
):
    c, s = lax.axis_index("ctx"), lax.axis_index("sub")
    rows, span = q.shape[0], k.shape[0]
    heads = k.shape[1] // HD
    guests = guest_q.shape[0]
    kept = heads - guests
    helper, last = c == n - 2, c == n - 1
    part = span // subs
    group = q.shape[1] // k.shape[1]
    image_rows = img.shape[2]
    mine = c * subs + s

    def sibling(d):
        return {"sub": lax.rem(s + d, subs)}

    barrier = pltpu.get_barrier_semaphore()

    @pl.loop(1, n)
    def _(d):
        pl.semaphore_signal(barrier, inc=1, device_id={"ctx": lax.rem(c + d, n)}, device_id_type=MESH)

    for d in range(1, subs):
        pl.semaphore_signal(barrier, inc=1, device_id=sibling(d), device_id_type=MESH)

    loads = [
        pltpu.make_async_copy(src, dst, in_sem.at[i])
        for i, (src, dst) in enumerate(
            [
                (k_hbm, k), (v_hbm, v), (ik_hbm, img.at[mine, 0]), (iv_hbm, img.at[mine, 1]),
                (q_hbm, q), (len_hbm, lengths), (tok_hbm, tokens),
            ]
        )
    ]
    for load in loads:
        load.start()

    def lay_out(ss):
        for j in range(heads):
            cols = slice(j * HD, (j + 1) * HD)
            kv[c, j, ss, 0] = k[pl.ds(ss * part, part), cols]
            for i in range(0, part, HD):
                kv[c, j, ss, 1, i:i + HD] = v[pl.ds(ss * part + i, HD), cols].T

    loads[0].wait()
    loads[1].wait()
    lay_out(s)
    loads[2].wait()
    loads[3].wait()
    pl.semaphore_wait(barrier, n - 1 + subs - 1)

    def up(b, j):
        return pltpu.make_async_remote_copy(
            kv.at[b, j, s], kv.at[b, j, s], up_send.at[b, j], text_recv.at[b, j, s],
            device_id={"ctx": lax.rem(c + 1, n)}, device_id_type=MESH,
        )

    def side(b, j, ss, d):
        return pltpu.make_async_remote_copy(
            kv.at[b, j, ss], kv.at[b, j, ss], side_send.at[b, j, d - 1], text_recv.at[b, j, ss],
            device_id=sibling(d), device_id_type=MESH,
        )

    def image_up(cc):
        at = cc * subs + s
        return pltpu.make_async_remote_copy(
            img.at[at], img.at[at], img_up.at[cc], img_recv.at[at],
            device_id={"ctx": lax.rem(c + 1, n)}, device_id_type=MESH,
        )

    def image_down(cc):
        at = cc * subs + s
        return pltpu.make_async_remote_copy(
            img.at[at], img.at[at], img_down.at[cc], img_recv.at[at],
            device_id={"ctx": lax.rem(c + n - 1, n)}, device_id_type=MESH,
        )

    def query_down(i):
        return pltpu.make_async_remote_copy(
            qt.at[kept + i], guest_q.at[i], q_send.at[i], q_recv.at[i],
            device_id={"ctx": lax.rem(c + n - 1, n)}, device_id_type=MESH,
        )

    def part_up(i):
        return [
            pltpu.make_async_remote_copy(
                ref.at[i], ref.at[i], part_send.at[i, e], part_recv.at[i, e],
                device_id={"ctx": lax.rem(c + 1, n)}, device_id_type=MESH,
            )
            for e, ref in enumerate([part_stats, part_out])
        ]

    def image_side(cc, ss, d):
        at = cc * subs + ss
        return pltpu.make_async_remote_copy(
            img.at[at], img.at[at], img_side.at[cc, d - 1], img_recv.at[at],
            device_id=sibling(d), device_id_type=MESH,
        )

    @pl.when(c < n - 1)
    def _():
        image_up(c).start()
        for j in range(kept):
            up(c, j).start()

    @pl.when(c > 0)
    def _():
        image_down(c).start()

    for d in range(1, subs):
        image_side(c, s, d).start()

    for d in range(1, subs):
        lay_out(lax.rem(s + d, subs))
    loads[4].wait()
    for j in range(heads):
        for g in range(group):
            h = j * group + g
            qt[j, :, g * rows:(g + 1) * rows] = q[:, h * HD:(h + 1) * HD].T

    @pl.when(last)
    def _():
        for i in range(guests):
            query_down(i).start()

    def scores(query, key_rows):
        return jnp.dot(key_rows, query, preferred_element_type=jnp.float32) * SCALE

    def wide(x):
        return jnp.concatenate([x] * group, axis=1)

    def put(ref, j, out):
        out = out.astype(jnp.bfloat16)
        for g in range(group):
            at = (j * group + g) * HD
            if not isinstance(at, int):
                at = pl.multiple_of(at, HD)
            ref[:, pl.ds(at, HD)] = out[:, g * rows:(g + 1) * rows].T

    def keys_of(b, j):
        return jnp.concatenate([kv[b, j, ss, 0] for ss in range(subs)], axis=0)

    def values_of(b, j):
        return jnp.concatenate(
            [kv[b, j, ss, 1, i:i + HD] for ss in range(subs) for i in range(0, part, HD)], axis=1
        )

    def finish(j):
        put(self_ref, j, run_out[j] * (1.0 / run_sum[j]))

    def image_step(d):
        @pl.when(c >= d)
        def _():
            cc = c - d
            image_up(cc).wait_recv()

            @pl.when(c < n - 1)
            def _():
                image_up(cc).start()

            for e in range(1, subs):
                image_side(cc, s, e).start()

        @pl.when(c + d < n)
        def _():
            cc = c + d
            image_down(cc).wait_recv()

            @pl.when(c > 0)
            def _():
                image_down(cc).start()

            for e in range(1, subs):
                image_side(cc, s, e).start()

    key_at = lax.broadcasted_iota(jnp.int32, (span, rows), 0)
    row_at = lax.broadcasted_iota(jnp.int32, (span, rows), 1) + s * rows
    bias = wide(jnp.where(key_at <= row_at, 0.0, LOW))
    for j in range(heads):
        sc = scores(qt[j], keys_of(c, j)) + bias
        top = jnp.max(sc, axis=0, keepdims=True)
        w = jnp.exp2(sc - top)
        run_max[j] = top
        run_sum[j] = jnp.sum(w, axis=0, keepdims=True)
        run_out[j] = jnp.dot(values_of(c, j), w.astype(jnp.bfloat16), preferred_element_type=jnp.float32)
        if j + 1 < n:
            image_step(j + 1)

    if heads + 1 < n:
        @pl.loop(heads + 1, n)
        def _(d):
            image_step(d)

    @pl.when(c == 0)
    def _():
        for j in range(heads):
            finish(j)

    def update(key_rows, value_cols, query, maxes, sums, outs, i):
        sc = scores(query, key_rows)
        old = maxes[i]
        top = jnp.maximum(old, jnp.max(sc, axis=0, keepdims=True))
        w = jnp.exp2(sc - top)
        factor = jnp.exp2(old - top)
        maxes[i] = top
        sums[i] = sums[i] * factor + jnp.sum(w, axis=0, keepdims=True)
        outs[i] = outs[i] * factor + jnp.dot(
            value_cols, w.astype(jnp.bfloat16), preferred_element_type=jnp.float32
        )

    def attend(b, j):
        update(keys_of(b, j), values_of(b, j), qt[j], run_max, run_sum, run_out, j)

        @pl.when(b == 0)
        def _():
            finish(j)

    def attend_guest(b, i):
        j = kept + i
        update(keys_of(b, j), values_of(b, j), guest_q[i], guest_max, guest_sum, guest_out, i)

        @pl.when(b == 0)
        def _():
            part_out[i] = (guest_out[i] * (1.0 / guest_sum[i])).astype(jnp.bfloat16)
            part_stats[i, 0:1] = guest_max[i]
            part_stats[i, 1:2] = guest_sum[i]
            for copy in part_up(i):
                copy.start()

    def await_siblings(b, j):
        for d in range(1, subs):
            side(b, j, lax.rem(s + d, subs), d).wait_recv()

    def pass_on(b, j, onward):
        up(b, j).wait_recv()

        @pl.when(onward)
        def _():
            up(b, j).start()

        for d in range(1, subs):
            side(b, j, s, d).start()

    def place(x):
        return c - 1 - lax.div(x, kept), lax.rem(x, kept)

    @pl.loop(0, c * kept + jnp.where(c > 0, 1, 0))
    def _(x):
        @pl.when(x < c * kept)
        def _():
            pass_on(*place(x), c < n - 1)

        @pl.when(x > 0)
        def _():
            b, j = place(x - 1)
            await_siblings(b, j)
            attend(b, j)

    @pl.when(c < n - 2)
    def _():
        up(c, kept).start()

    @pl.when(helper)
    def _():
        for i in range(guests):
            query_down(i).wait_recv()
            guest_max[i] = jnp.full(guest_max.shape[1:], LOW, jnp.float32)
            guest_sum[i] = jnp.zeros(guest_sum.shape[1:], jnp.float32)
            guest_out[i] = jnp.zeros(guest_out.shape[1:], jnp.float32)
            attend_guest(c, i)

    @pl.when(jnp.logical_and(c == 0, c < n - 2))
    def _():
        for i in range(1, guests):
            up(c, kept + i).start()

    turns = jnp.where(last, 0, c * guests)

    def guest_place(y):
        return c - 1 - lax.rem(y, jnp.maximum(c, 1)), lax.div(y, jnp.maximum(c, 1))

    @pl.loop(0, turns + jnp.where(turns > 0, 1, 0))
    def _(y):
        @pl.when(y < turns)
        def _():
            b, i = guest_place(y)
            pass_on(b, kept + i, c < n - 2)

            @pl.when(jnp.logical_and(c < n - 2, jnp.logical_and(b == 0, i + 1 < guests)))
            def _():
                up(c, kept + i + 1).start()

        @pl.when(y > 0)
        def _():
            b, i = guest_place(y - 1)
            attend(b, kept + i)

        @pl.when(y < turns)
        def _():
            b, i = guest_place(y)
            await_siblings(b, kept + i)

            @pl.when(helper)
            def _():
                attend_guest(b, i)

    @pl.loop(0, n)
    def _(cc):
        for e in range(1, subs):
            image_side(cc, lax.rem(s + e, subs), e).wait_recv()

    loads[5].wait()
    loads[6].wait()
    seen_images = tokens[pl.ds(mine, 1), :]
    visible = jnp.zeros_like(seen_images)
    for i in range(lengths.shape[0]):
        visible = visible + jnp.where(seen_images > i, lengths[i], 0)
    visible = wide(visible)
    count = n * subs * image_rows
    allowed = lax.broadcasted_iota(jnp.int32, (count, group * rows), 0) < visible
    for j in range(heads):
        cols = slice(j * HD, (j + 1) * HD)
        sc = jnp.where(allowed, scores(qt[j], img[:, 0, :, cols].reshape(count, HD)), LOW)
        top = jnp.max(sc, axis=0, keepdims=True)
        w = jnp.where(allowed, jnp.exp2(sc - top), 0.0)
        total = jnp.sum(w, axis=0, keepdims=True)
        out = jnp.dot(
            img[:, 1, :, cols].reshape(count, HD).T, w.astype(jnp.bfloat16),
            preferred_element_type=jnp.float32,
        )
        out = jnp.where(visible > 0, out * (1.0 / jnp.where(visible > 0, total, 1.0)), 0.0)
        put(cross_ref, j, out)

    @pl.when(last)
    def _():
        for i in range(guests):
            j = kept + i
            for copy in part_up(i):
                copy.wait_recv()
            their_max, their_sum = part_stats[i, 0:1], part_stats[i, 1:2]
            top = jnp.maximum(run_max[j], their_max)
            factor = jnp.exp2(run_max[j] - top)
            weight = their_sum * jnp.exp2(their_max - top)
            scale = 1.0 / (run_sum[j] * factor + weight)
            out = run_out[j] * (factor * scale) + part_out[i].astype(jnp.float32) * (weight * scale)
            put(self_ref, j, out)

    @pl.loop(0, n)
    def _(cc):
        @pl.when(jnp.logical_and(cc <= c, c < n - 1))
        def _():
            image_up(cc).wait_send()

        @pl.when(jnp.logical_and(cc >= c, c > 0))
        def _():
            image_down(cc).wait_send()

        for d in range(1, subs):
            image_side(cc, s, d).wait_send()

    @pl.loop(0, c + 1)
    def _(b):
        for j in range(heads):
            @pl.when(c < (n - 1 if j < kept else n - 2))
            def _():
                up(b, j).wait_send()

            @pl.when(jnp.logical_and(b < c, c < (n if j < kept else n - 1)))
            def _():
                for d in range(1, subs):
                    side(b, j, s, d).wait_send()

    for i in range(guests):
        @pl.when(last)
        def _():
            query_down(i).wait_send()

        @pl.when(helper)
        def _():
            for copy in part_up(i):
                copy.wait_send()


def local(queries, keys, values, image_keys, image_values, image_lengths, token_images):
    n, subs = lax.axis_size("ctx"), lax.axis_size("sub")
    rows, wide = queries.shape
    span, narrow = keys.shape
    heads, image_rows = narrow // HD, image_keys.shape[0]
    group = wide // narrow
    guests = heads // 2
    vmem = pl.BlockSpec(memory_space=pltpu.VMEM)
    hbm = pl.BlockSpec(memory_space=pltpu.HBM)
    dma = pltpu.SemaphoreType.DMA
    out = pltpu.VMEM((rows, wide), jnp.bfloat16)
    token_images = token_images.reshape(-1, rows)
    return pl.pallas_call(
        functools.partial(kernel, n, subs),
        out_shape=(out, out),
        in_specs=[hbm] * 7,
        out_specs=(vmem, vmem),
        scratch_shapes=[
            pltpu.SMEM(image_lengths.shape, jnp.int32),
            pltpu.VMEM(token_images.shape, jnp.int32),
            pltpu.VMEM((rows, wide), jnp.bfloat16),
            pltpu.VMEM((span, narrow), jnp.bfloat16),
            pltpu.VMEM((span, narrow), jnp.bfloat16),
            pltpu.VMEM((heads, HD, group * rows), jnp.bfloat16),
            pltpu.VMEM((n, heads, subs, 2, span // subs, HD), jnp.bfloat16),
            pltpu.VMEM((n * subs, 2, image_rows, narrow), jnp.bfloat16),
            pltpu.VMEM((heads, 1, group * rows), jnp.float32),
            pltpu.VMEM((heads, 1, group * rows), jnp.float32),
            pltpu.VMEM((heads, HD, group * rows), jnp.float32),
            pltpu.VMEM((guests, HD, group * rows), jnp.bfloat16),
            pltpu.VMEM((guests, 1, group * rows), jnp.float32),
            pltpu.VMEM((guests, 1, group * rows), jnp.float32),
            pltpu.VMEM((guests, HD, group * rows), jnp.float32),
            pltpu.VMEM((guests, HD, group * rows), jnp.bfloat16),
            pltpu.VMEM((guests, 2, group * rows), jnp.float32),
            dma((7,)),
            dma((n, heads, subs)),
            dma((n, heads)),
            dma((n, heads, subs - 1)),
            dma((n * subs,)),
            dma((n,)),
            dma((n,)),
            dma((n, subs - 1)),
            dma((guests,)),
            dma((guests,)),
            dma((guests, 2)),
            dma((guests, 2)),
        ],
        compiler_params=pltpu.CompilerParams(
            collective_id=0, has_side_effects=True, vmem_limit_bytes=60 * 1024 * 1024
        ),
    )(image_lengths, token_images, queries, keys, values, image_keys, image_values)


def solution(mesh):
    fine = P(("groups", "ctx", "sub"), "heads")
    block = P(("groups", "ctx"), "heads")
    in_specs = (fine, block, block, fine, fine, P("groups"), P("groups"))
    return jax.shard_map(local, mesh=mesh, in_specs=in_specs, out_specs=(fine, fine), check_vma=False)
```

```python
import functools
import math

import jax
import jax.numpy as jnp
from jax import lax
from jax.experimental import pallas as pl
from jax.experimental.pallas import tpu as pltpu
from jax.sharding import PartitionSpec as P

HD = 128
MESH = pl.DeviceIdType.MESH
LOW = -1e30
SCALE = math.log2(math.e) / math.sqrt(HD)


def kernel(
    n, subs, len_hbm, tok_hbm, q_hbm, k_hbm, v_hbm, ik_hbm, iv_hbm, self_ref, cross_ref,
    lengths, tokens, q, k, v, qt, kv, img, run_max, run_sum, run_out,
    in_sem, text_recv, up_send, side_send, img_recv, img_send, img_side,
):
    c, s = lax.axis_index("ctx"), lax.axis_index("sub")
    rows, span = q.shape[0], k.shape[0]
    heads = k.shape[1] // HD
    part = span // subs
    group = q.shape[1] // k.shape[1]
    image_rows = img.shape[2]
    mine = c * subs + s

    def sibling(d):
        return {"sub": lax.rem(s + d, subs)}

    barrier = pltpu.get_barrier_semaphore()

    @pl.loop(1, n)
    def _(d):
        pl.semaphore_signal(barrier, inc=1, device_id={"ctx": lax.rem(c + d, n)}, device_id_type=MESH)

    for d in range(1, subs):
        pl.semaphore_signal(barrier, inc=1, device_id=sibling(d), device_id_type=MESH)

    loads = [
        pltpu.make_async_copy(src, dst, in_sem.at[i])
        for i, (src, dst) in enumerate(
            [
                (k_hbm, k), (v_hbm, v), (ik_hbm, img.at[mine, 0]), (iv_hbm, img.at[mine, 1]),
                (q_hbm, q), (len_hbm, lengths), (tok_hbm, tokens),
            ]
        )
    ]
    for load in loads:
        load.start()

    def lay_out(ss):
        for j in range(heads):
            cols = slice(j * HD, (j + 1) * HD)
            kv[c, j, ss, 0] = k[pl.ds(ss * part, part), cols]
            for i in range(0, part, HD):
                kv[c, j, ss, 1, i:i + HD] = v[pl.ds(ss * part + i, HD), cols].T

    loads[0].wait()
    loads[1].wait()
    lay_out(s)
    loads[2].wait()
    loads[3].wait()
    pl.semaphore_wait(barrier, n - 1 + subs - 1)

    def up(b, j):
        return pltpu.make_async_remote_copy(
            kv.at[b, j, s], kv.at[b, j, s], up_send.at[b, j], text_recv.at[b, j, s],
            device_id={"ctx": lax.rem(c + 1, n)}, device_id_type=MESH,
        )

    def side(b, j, ss, d):
        return pltpu.make_async_remote_copy(
            kv.at[b, j, ss], kv.at[b, j, ss], side_send.at[b, j, d - 1], text_recv.at[b, j, ss],
            device_id=sibling(d), device_id_type=MESH,
        )

    def image_to(d):
        return pltpu.make_async_remote_copy(
            img.at[mine], img.at[mine], img_send.at[d - 1], img_recv.at[mine],
            device_id={"ctx": lax.rem(c + d, n)}, device_id_type=MESH,
        )

    def image_side(cc, ss, d):
        at = cc * subs + ss
        return pltpu.make_async_remote_copy(
            img.at[at], img.at[at], img_side.at[cc, d - 1], img_recv.at[at],
            device_id=sibling(d), device_id_type=MESH,
        )

    @pl.loop(1, n)
    def _(d):
        image_to(d).start()

    for d in range(1, subs):
        image_side(c, s, d).start()

    @pl.when(c < n - 1)
    def _():
        for j in range(heads):
            up(c, j).start()

    for d in range(1, subs):
        lay_out(lax.rem(s + d, subs))
    loads[4].wait()
    for j in range(heads):
        for g in range(group):
            h = j * group + g
            qt[j, :, g * rows:(g + 1) * rows] = q[:, h * HD:(h + 1) * HD].T

    def scores(j, key_rows):
        return jnp.dot(key_rows, qt[j], preferred_element_type=jnp.float32) * SCALE

    def wide(x):
        return jnp.concatenate([x] * group, axis=1)

    def put(ref, j, out):
        out = out.astype(jnp.bfloat16)
        for g in range(group):
            at = (j * group + g) * HD
            if not isinstance(at, int):
                at = pl.multiple_of(at, HD)
            ref[:, pl.ds(at, HD)] = out[:, g * rows:(g + 1) * rows].T

    def keys_of(b, j):
        return jnp.concatenate([kv[b, j, ss, 0] for ss in range(subs)], axis=0)

    def values_of(b, j):
        return jnp.concatenate(
            [kv[b, j, ss, 1, i:i + HD] for ss in range(subs) for i in range(0, part, HD)], axis=1
        )

    def finish(j):
        put(self_ref, j, run_out[j] * (1.0 / run_sum[j]))

    key_at = lax.broadcasted_iota(jnp.int32, (span, rows), 0)
    row_at = lax.broadcasted_iota(jnp.int32, (span, rows), 1) + s * rows
    bias = wide(jnp.where(key_at <= row_at, 0.0, LOW))
    batch = 2 if heads % 2 == 0 else 1
    for first in range(0, heads, batch):
        js = range(first, first + batch)
        scs = [scores(j, keys_of(c, j)) + bias for j in js]
        tops = [jnp.max(sc, axis=0, keepdims=True) for sc in scs]
        ws = [jnp.exp2(sc - top) for sc, top in zip(scs, tops)]
        sums = [jnp.sum(w, axis=0, keepdims=True) for w in ws]
        outs = [
            jnp.dot(values_of(c, j), w.astype(jnp.bfloat16), preferred_element_type=jnp.float32)
            for j, w in zip(js, ws)
        ]
        for j, top, total, out in zip(js, tops, sums, outs):
            run_max[j], run_sum[j], run_out[j] = top, total, out

    @pl.when(c == 0)
    def _():
        for j in range(heads):
            finish(j)

    @pl.loop(1, n)
    def _(d):
        cc = lax.rem(c + d, n)
        image_side(cc, s, 1).wait_recv()
        for e in range(1, subs):
            image_side(cc, s, e).start()

    @pl.loop(0, n)
    def _(cc):
        for e in range(1, subs):
            image_side(cc, lax.rem(s + e, subs), e).wait_recv()

    loads[5].wait()
    loads[6].wait()
    seen_images = tokens[pl.ds(mine, 1), :]
    visible = jnp.zeros_like(seen_images)
    for i in range(lengths.shape[0]):
        visible = visible + jnp.where(seen_images > i, lengths[i], 0)
    visible = wide(visible)
    count = n * subs * image_rows
    allowed = lax.broadcasted_iota(jnp.int32, (count, group * rows), 0) < visible
    for j in range(heads):
        cols = slice(j * HD, (j + 1) * HD)
        sc = jnp.where(allowed, scores(j, img[:, 0, :, cols].reshape(count, HD)), LOW)
        top = jnp.max(sc, axis=0, keepdims=True)
        w = jnp.where(allowed, jnp.exp2(sc - top), 0.0)
        total = jnp.sum(w, axis=0, keepdims=True)
        out = jnp.dot(
            img[:, 1, :, cols].reshape(count, HD).T, w.astype(jnp.bfloat16),
            preferred_element_type=jnp.float32,
        )
        out = jnp.where(visible > 0, out * (1.0 / jnp.where(visible > 0, total, 1.0)), 0.0)
        put(cross_ref, j, out)

    def attend(b, first):
        js = [first + i for i in range(batch)]
        olds, totals, accs = [run_max[j] for j in js], [run_sum[j] for j in js], [run_out[j] for j in js]
        scs = [scores(j, keys_of(b, j)) for j in js]
        cols = [values_of(b, j) for j in js]
        tops = [jnp.maximum(old, jnp.max(sc, axis=0, keepdims=True)) for old, sc in zip(olds, scs)]
        ws = [jnp.exp2(sc - top) for sc, top in zip(scs, tops)]
        factors = [jnp.exp2(old - top) for old, top in zip(olds, tops)]
        totals = [
            total * factor + jnp.sum(w, axis=0, keepdims=True)
            for total, factor, w in zip(totals, factors, ws)
        ]
        accs = [
            acc * factor + jnp.dot(col, w.astype(jnp.bfloat16), preferred_element_type=jnp.float32)
            for acc, factor, col, w in zip(accs, factors, cols, ws)
        ]

        @pl.when(b > 0)
        def _():
            for j, top, total, acc in zip(js, tops, totals, accs):
                run_max[j], run_sum[j], run_out[j] = top, total, acc

        @pl.when(b == 0)
        def _():
            for j, total, acc in zip(js, totals, accs):
                put(self_ref, j, acc * (1.0 / total))

    turns = c * heads // batch

    def place(x):
        return c - 1 - lax.div(x * batch, heads), lax.rem(x * batch, heads)

    def receive(x):
        b, first = place(x)
        for i in range(batch):
            up(b, first + i).wait_recv()

            @pl.when(c < n - 1)
            def _():
                up(b, first + i).start()

            for d in range(1, subs):
                side(b, first + i, s, d).start()

    def consume(x):
        b, first = place(x)
        for i in range(batch):
            for d in range(1, subs):
                side(b, first + i, lax.rem(s + d, subs), d).wait_recv()
        attend(b, first)

    @pl.when(c > 0)
    def _():
        @pl.when(turns > 1)
        def _():
            receive(jnp.int32(0))

        @pl.loop(1, turns - 1)
        def _(x):
            receive(x)
            consume(x - 1)

        @pl.when(turns > 1)
        def _():
            consume(turns - 2)

        receive(turns - 1)
        consume(turns - 1)

    @pl.loop(1, n)
    def _(d):
        image_to(d).wait_send()

    @pl.loop(0, n)
    def _(cc):
        for d in range(1, subs):
            image_side(cc, s, d).wait_send()

    @pl.when(c < n - 1)
    def _():
        @pl.loop(0, c + 1)
        def _(b):
            for j in range(heads):
                up(b, j).wait_send()

    @pl.loop(0, c)
    def _(b):
        for j in range(heads):
            for d in range(1, subs):
                side(b, j, s, d).wait_send()


def local(queries, keys, values, image_keys, image_values, image_lengths, token_images):
    n, subs = lax.axis_size("ctx"), lax.axis_size("sub")
    rows, wide = queries.shape
    span, narrow = keys.shape
    heads, image_rows = narrow // HD, image_keys.shape[0]
    group = wide // narrow
    vmem = pl.BlockSpec(memory_space=pltpu.VMEM)
    hbm = pl.BlockSpec(memory_space=pltpu.HBM)
    dma = pltpu.SemaphoreType.DMA
    out = pltpu.VMEM((rows, wide), jnp.bfloat16)
    token_images = token_images.reshape(-1, rows)
    return pl.pallas_call(
        functools.partial(kernel, n, subs),
        out_shape=(out, out),
        in_specs=[hbm] * 7,
        out_specs=(vmem, vmem),
        scratch_shapes=[
            pltpu.SMEM(image_lengths.shape, jnp.int32),
            pltpu.VMEM(token_images.shape, jnp.int32),
            pltpu.VMEM((rows, wide), jnp.bfloat16),
            pltpu.VMEM((span, narrow), jnp.bfloat16),
            pltpu.VMEM((span, narrow), jnp.bfloat16),
            pltpu.VMEM((heads, HD, group * rows), jnp.bfloat16),
            pltpu.VMEM((n, heads, subs, 2, span // subs, HD), jnp.bfloat16),
            pltpu.VMEM((n * subs, 2, image_rows, narrow), jnp.bfloat16),
            pltpu.VMEM((heads, 1, group * rows), jnp.float32),
            pltpu.VMEM((heads, 1, group * rows), jnp.float32),
            pltpu.VMEM((heads, HD, group * rows), jnp.float32),
            dma((7,)),
            dma((n, heads, subs)),
            dma((n, heads)),
            dma((n, heads, subs - 1)),
            dma((n * subs,)),
            dma((n - 1,)),
            dma((n, subs - 1)),
        ],
        compiler_params=pltpu.CompilerParams(
            collective_id=0, has_side_effects=True, vmem_limit_bytes=60 * 1024 * 1024
        ),
    )(image_lengths, token_images, queries, keys, values, image_keys, image_values)


def solution(mesh):
    fine = P(("groups", "ctx", "sub"), "heads")
    block = P(("groups", "ctx"), "heads")
    in_specs = (fine, block, block, fine, fine, P("groups"), P("groups"))
    return jax.shard_map(local, mesh=mesh, in_specs=in_specs, out_specs=(fine, fine), check_vma=False)
```

```python
import functools
import math

import jax
import jax.numpy as jnp
from jax import lax
from jax.experimental import pallas as pl
from jax.experimental.pallas import tpu as pltpu
from jax.sharding import PartitionSpec as P

HD = 128
MESH = pl.DeviceIdType.MESH
LOW = -1e30
SCALE = math.log2(math.e) / math.sqrt(HD)


def kernel(
    n, subs, len_hbm, tok_hbm, q_hbm, k_hbm, v_hbm, ik_hbm, iv_hbm, self_ref, cross_ref,
    lengths, tokens, q, k, v, qt, kv, img, run_max, run_sum, run_out,
    in_sem, text_recv, up_send, side_send, img_recv, img_send, img_side,
):
    c, s = lax.axis_index("ctx"), lax.axis_index("sub")
    rows, span = q.shape[0], k.shape[0]
    heads = k.shape[1] // HD
    part = span // subs
    group = q.shape[1] // k.shape[1]
    image_rows = img.shape[2]
    mine = c * subs + s

    def sibling(d):
        return {"sub": lax.rem(s + d, subs)}

    barrier = pltpu.get_barrier_semaphore()

    @pl.loop(1, n)
    def _(d):
        pl.semaphore_signal(barrier, inc=1, device_id={"ctx": lax.rem(c + d, n)}, device_id_type=MESH)

    for d in range(1, subs):
        pl.semaphore_signal(barrier, inc=1, device_id=sibling(d), device_id_type=MESH)

    loads = [
        pltpu.make_async_copy(src, dst, in_sem.at[i])
        for i, (src, dst) in enumerate(
            [
                (k_hbm, k), (v_hbm, v), (ik_hbm, img.at[mine, 0]), (iv_hbm, img.at[mine, 1]),
                (q_hbm, q), (len_hbm, lengths), (tok_hbm, tokens),
            ]
        )
    ]
    for load in loads:
        load.start()

    def lay_out(ss):
        for j in range(heads):
            cols = slice(j * HD, (j + 1) * HD)
            kv[c, j, ss, 0] = k[pl.ds(ss * part, part), cols]
            for i in range(0, part, HD):
                kv[c, j, ss, 1, i:i + HD] = v[pl.ds(ss * part + i, HD), cols].T

    loads[0].wait()
    loads[1].wait()
    lay_out(s)
    loads[2].wait()
    loads[3].wait()
    pl.semaphore_wait(barrier, n - 1 + subs - 1)

    def up(b, j):
        return pltpu.make_async_remote_copy(
            kv.at[b, j, s], kv.at[b, j, s], up_send.at[b, j], text_recv.at[b, j, s],
            device_id={"ctx": lax.rem(c + 1, n)}, device_id_type=MESH,
        )

    def side(b, j, ss, d):
        return pltpu.make_async_remote_copy(
            kv.at[b, j, ss], kv.at[b, j, ss], side_send.at[b, j, d - 1], text_recv.at[b, j, ss],
            device_id=sibling(d), device_id_type=MESH,
        )

    def image_to(d):
        return pltpu.make_async_remote_copy(
            img.at[mine], img.at[mine], img_send.at[d - 1], img_recv.at[mine],
            device_id={"ctx": lax.rem(c + d, n)}, device_id_type=MESH,
        )

    def image_side(cc, ss, d):
        at = cc * subs + ss
        return pltpu.make_async_remote_copy(
            img.at[at], img.at[at], img_side.at[cc, d - 1], img_recv.at[at],
            device_id=sibling(d), device_id_type=MESH,
        )

    @pl.loop(1, n)
    def _(d):
        image_to(d).start()

    for d in range(1, subs):
        image_side(c, s, d).start()

    @pl.when(c < n - 1)
    def _():
        for j in range(heads):
            up(c, j).start()

    for d in range(1, subs):
        lay_out(lax.rem(s + d, subs))
    loads[4].wait()
    for j in range(heads):
        for g in range(group):
            h = j * group + g
            qt[j, :, g * rows:(g + 1) * rows] = q[:, h * HD:(h + 1) * HD].T

    def scores(j, key_rows):
        return jnp.dot(key_rows, qt[j], preferred_element_type=jnp.float32) * SCALE

    def wide(x):
        return jnp.concatenate([x] * group, axis=1)

    def put(ref, j, out):
        out = out.astype(jnp.bfloat16)
        for g in range(group):
            at = (j * group + g) * HD
            if not isinstance(at, int):
                at = pl.multiple_of(at, HD)
            ref[:, pl.ds(at, HD)] = out[:, g * rows:(g + 1) * rows].T

    def keys_of(b, j):
        return jnp.concatenate([kv[b, j, ss, 0] for ss in range(subs)], axis=0)

    def values_of(b, j):
        return jnp.concatenate(
            [kv[b, j, ss, 1, i:i + HD] for ss in range(subs) for i in range(0, part, HD)], axis=1
        )

    def finish(j):
        put(self_ref, j, run_out[j] * (1.0 / run_sum[j]))

    key_at = lax.broadcasted_iota(jnp.int32, (span, rows), 0)
    row_at = lax.broadcasted_iota(jnp.int32, (span, rows), 1) + s * rows
    bias = wide(jnp.where(key_at <= row_at, 0.0, LOW))
    batch = 2 if heads % 2 == 0 else 1
    for first in range(0, heads, batch):
        js = range(first, first + batch)
        scs = [scores(j, keys_of(c, j)) + bias for j in js]
        tops = [jnp.max(sc, axis=0, keepdims=True) for sc in scs]
        ws = [jnp.exp2(sc - top) for sc, top in zip(scs, tops)]
        sums = [jnp.sum(w, axis=0, keepdims=True) for w in ws]
        outs = [
            jnp.dot(values_of(c, j), w.astype(jnp.bfloat16), preferred_element_type=jnp.float32)
            for j, w in zip(js, ws)
        ]
        for j, top, total, out in zip(js, tops, sums, outs):
            run_max[j], run_sum[j], run_out[j] = top, total, out

    @pl.when(c == 0)
    def _():
        for j in range(heads):
            finish(j)

    @pl.loop(1, n)
    def _(d):
        cc = lax.rem(c + d, n)
        image_side(cc, s, 1).wait_recv()
        for e in range(1, subs):
            image_side(cc, s, e).start()

    @pl.loop(0, n)
    def _(cc):
        for e in range(1, subs):
            image_side(cc, lax.rem(s + e, subs), e).wait_recv()

    turns = c * heads // batch

    def place(x):
        return c - 1 - lax.div(x * batch, heads), lax.rem(x * batch, heads)

    def receive_head(b, j):
        up(b, j).wait_recv()

        @pl.when(c < n - 1)
        def _():
            up(b, j).start()

        for d in range(1, subs):
            side(b, j, s, d).start()

    def await_siblings(b, j):
        for d in range(1, subs):
            side(b, j, lax.rem(s + d, subs), d).wait_recv()

    def receive(x):
        b, first = place(x)
        for i in range(batch):
            receive_head(b, first + i)

    def consume(x):
        b, first = place(x)
        js = [first + i for i in range(batch)]
        for j in js:
            await_siblings(b, j)
        attend([(j, keys_of(b, j), values_of(b, j)) for j in js])

        @pl.when(b == 0)
        def _():
            for j in js:
                finish(j)

    @pl.when(turns > 1)
    def _():
        receive(jnp.int32(0))

    loads[5].wait()
    loads[6].wait()
    seen_images = tokens[pl.ds(mine, 1), :]
    visible = jnp.zeros_like(seen_images)
    for i in range(lengths.shape[0]):
        visible = visible + jnp.where(seen_images > i, lengths[i], 0)
    visible = wide(visible)
    count = n * subs * image_rows
    allowed = lax.broadcasted_iota(jnp.int32, (count, group * rows), 0) < visible
    for j in range(heads):
        cols = slice(j * HD, (j + 1) * HD)
        sc = jnp.where(allowed, scores(j, img[:, 0, :, cols].reshape(count, HD)), LOW)
        top = jnp.max(sc, axis=0, keepdims=True)
        w = jnp.where(allowed, jnp.exp2(sc - top), 0.0)
        total = jnp.sum(w, axis=0, keepdims=True)
        out = jnp.dot(
            img[:, 1, :, cols].reshape(count, HD).T, w.astype(jnp.bfloat16),
            preferred_element_type=jnp.float32,
        )
        out = jnp.where(visible > 0, out * (1.0 / jnp.where(visible > 0, total, 1.0)), 0.0)
        put(cross_ref, j, out)

    def attend(items):
        js = [j for j, _, _ in items]
        olds, totals, accs = [run_max[j] for j in js], [run_sum[j] for j in js], [run_out[j] for j in js]
        scs = [scores(j, key_rows) for j, key_rows, _ in items]
        tops = [jnp.maximum(old, jnp.max(sc, axis=0, keepdims=True)) for old, sc in zip(olds, scs)]
        ws = [jnp.exp2(sc - top) for sc, top in zip(scs, tops)]
        factors = [jnp.exp2(old - top) for old, top in zip(olds, tops)]
        totals = [
            total * factor + jnp.sum(w, axis=0, keepdims=True)
            for total, factor, w in zip(totals, factors, ws)
        ]
        accs = [
            acc * factor + jnp.dot(cols, w.astype(jnp.bfloat16), preferred_element_type=jnp.float32)
            for acc, factor, (_, _, cols), w in zip(accs, factors, items, ws)
        ]
        for j, top, total, acc in zip(js, tops, totals, accs):
            run_max[j], run_sum[j], run_out[j] = top, total, acc

    def attend_part(b, j, ss):
        cols = jnp.concatenate([kv[b, j, ss, 1, i:i + HD] for i in range(0, part, HD)], axis=1)
        attend([(j, kv[b, j, ss, 0], cols)])

    @pl.when(c > 0)
    def _():
        @pl.loop(1, turns - 1)
        def _(x):
            receive(x)
            consume(x - 1)

        @pl.when(turns > 1)
        def _():
            consume(turns - 2)

        b, first = place(turns - 1)
        for i in range(batch):
            receive_head(b, first + i)
            if i > 0:
                finish(first + i - 1)
            attend_part(b, first + i, s)
            await_siblings(b, first + i)
            for d in range(1, subs):
                attend_part(b, first + i, lax.rem(s + d, subs))
        finish(first + batch - 1)

    @pl.loop(1, n)
    def _(d):
        image_to(d).wait_send()

    @pl.loop(0, n)
    def _(cc):
        for d in range(1, subs):
            image_side(cc, s, d).wait_send()

    @pl.when(c < n - 1)
    def _():
        @pl.loop(0, c + 1)
        def _(b):
            for j in range(heads):
                up(b, j).wait_send()

    @pl.loop(0, c)
    def _(b):
        for j in range(heads):
            for d in range(1, subs):
                side(b, j, s, d).wait_send()


def local(queries, keys, values, image_keys, image_values, image_lengths, token_images):
    n, subs = lax.axis_size("ctx"), lax.axis_size("sub")
    rows, wide = queries.shape
    span, narrow = keys.shape
    heads, image_rows = narrow // HD, image_keys.shape[0]
    group = wide // narrow
    vmem = pl.BlockSpec(memory_space=pltpu.VMEM)
    hbm = pl.BlockSpec(memory_space=pltpu.HBM)
    dma = pltpu.SemaphoreType.DMA
    out = pltpu.VMEM((rows, wide), jnp.bfloat16)
    token_images = token_images.reshape(-1, rows)
    return pl.pallas_call(
        functools.partial(kernel, n, subs),
        out_shape=(out, out),
        in_specs=[hbm] * 7,
        out_specs=(vmem, vmem),
        scratch_shapes=[
            pltpu.SMEM(image_lengths.shape, jnp.int32),
            pltpu.VMEM(token_images.shape, jnp.int32),
            pltpu.VMEM((rows, wide), jnp.bfloat16),
            pltpu.VMEM((span, narrow), jnp.bfloat16),
            pltpu.VMEM((span, narrow), jnp.bfloat16),
            pltpu.VMEM((heads, HD, group * rows), jnp.bfloat16),
            pltpu.VMEM((n, heads, subs, 2, span // subs, HD), jnp.bfloat16),
            pltpu.VMEM((n * subs, 2, image_rows, narrow), jnp.bfloat16),
            pltpu.VMEM((heads, 1, group * rows), jnp.float32),
            pltpu.VMEM((heads, 1, group * rows), jnp.float32),
            pltpu.VMEM((heads, HD, group * rows), jnp.float32),
            dma((7,)),
            dma((n, heads, subs)),
            dma((n, heads)),
            dma((n, heads, subs - 1)),
            dma((n * subs,)),
            dma((n - 1,)),
            dma((n, subs - 1)),
        ],
        compiler_params=pltpu.CompilerParams(
            collective_id=0, has_side_effects=True, vmem_limit_bytes=60 * 1024 * 1024
        ),
    )(image_lengths, token_images, queries, keys, values, image_keys, image_values)


def solution(mesh):
    fine = P(("groups", "ctx", "sub"), "heads")
    block = P(("groups", "ctx"), "heads")
    in_specs = (fine, block, block, fine, fine, P("groups"), P("groups"))
    return jax.shard_map(local, mesh=mesh, in_specs=in_specs, out_specs=(fine, fine), check_vma=False)
```

```python
import functools
import math

import jax
import jax.numpy as jnp
from jax import lax
from jax.experimental import pallas as pl
from jax.experimental.pallas import tpu as pltpu
from jax.sharding import PartitionSpec as P

HD = 128
MESH = pl.DeviceIdType.MESH
LOW = -1e30
SCALE = math.log2(math.e) / math.sqrt(HD)


def kernel(
    n, subs, len_hbm, tok_hbm, q_hbm, k_hbm, v_hbm, ik_hbm, iv_hbm, self_ref, cross_ref,
    lengths, tokens, q, k, v, qt, kv, img, run_max, run_sum, run_out,
    in_sem, text_recv, up_send, side_send, img_recv, img_send, img_side,
):
    c, s = lax.axis_index("ctx"), lax.axis_index("sub")
    rows, span = q.shape[0], k.shape[0]
    heads = k.shape[1] // HD
    part = span // subs
    group = q.shape[1] // k.shape[1]
    image_rows = img.shape[2]
    mine = c * subs + s

    def sibling(d):
        return {"sub": lax.rem(s + d, subs)}

    barrier = pltpu.get_barrier_semaphore()

    @pl.loop(1, n)
    def _(d):
        pl.semaphore_signal(barrier, inc=1, device_id={"ctx": lax.rem(c + d, n)}, device_id_type=MESH)

    for d in range(1, subs):
        pl.semaphore_signal(barrier, inc=1, device_id=sibling(d), device_id_type=MESH)

    loads = [
        pltpu.make_async_copy(src, dst, in_sem.at[i])
        for i, (src, dst) in enumerate(
            [
                (k_hbm, k), (v_hbm, v), (ik_hbm, img.at[mine, 0]), (iv_hbm, img.at[mine, 1]),
                (q_hbm, q), (len_hbm, lengths), (tok_hbm, tokens),
            ]
        )
    ]
    for load in loads:
        load.start()

    def lay_out(ss):
        for j in range(heads):
            cols = slice(j * HD, (j + 1) * HD)
            kv[c, j, ss, 0] = k[pl.ds(ss * part, part), cols]
            for i in range(0, part, HD):
                kv[c, j, ss, 1, i:i + HD] = v[pl.ds(ss * part + i, HD), cols].T

    loads[0].wait()
    loads[1].wait()
    lay_out(s)
    loads[2].wait()
    loads[3].wait()
    pl.semaphore_wait(barrier, n - 1 + subs - 1)

    def up(b, j):
        return pltpu.make_async_remote_copy(
            kv.at[b, j, s], kv.at[b, j, s], up_send.at[b, j], text_recv.at[b, j, s],
            device_id={"ctx": lax.rem(c + 1, n)}, device_id_type=MESH,
        )

    def side(b, j, ss, d):
        return pltpu.make_async_remote_copy(
            kv.at[b, j, ss], kv.at[b, j, ss], side_send.at[b, j, d - 1], text_recv.at[b, j, ss],
            device_id=sibling(d), device_id_type=MESH,
        )

    def image_to(d):
        return pltpu.make_async_remote_copy(
            img.at[mine], img.at[mine], img_send.at[d - 1], img_recv.at[mine],
            device_id={"ctx": lax.rem(c + d, n)}, device_id_type=MESH,
        )

    def image_side(cc, ss, d):
        at = cc * subs + ss
        return pltpu.make_async_remote_copy(
            img.at[at], img.at[at], img_side.at[cc, d - 1], img_recv.at[at],
            device_id=sibling(d), device_id_type=MESH,
        )

    @pl.loop(1, n)
    def _(d):
        image_to(d).start()

    for d in range(1, subs):
        image_side(c, s, d).start()

    @pl.when(c < n - 1)
    def _():
        for j in range(heads):
            up(c, j).start()

    for d in range(1, subs):
        lay_out(lax.rem(s + d, subs))
    loads[4].wait()
    for j in range(heads):
        for g in range(group):
            h = j * group + g
            qt[j, :, g * rows:(g + 1) * rows] = q[:, h * HD:(h + 1) * HD].T

    tiles = [slice(g * rows, (g + 1) * rows) for g in range(group)]

    def scores(j, key_rows, cols):
        return jnp.dot(key_rows, qt[j, :, cols], preferred_element_type=jnp.float32) * SCALE

    def put(ref, j, out):
        out = out.astype(jnp.bfloat16)
        for g in range(group):
            at = (j * group + g) * HD
            if not isinstance(at, int):
                at = pl.multiple_of(at, HD)
            ref[:, pl.ds(at, HD)] = out[:, g * rows:(g + 1) * rows].T

    def keys_of(b, j):
        return jnp.concatenate([kv[b, j, ss, 0] for ss in range(subs)], axis=0)

    def values_of(b, j):
        return jnp.concatenate(
            [kv[b, j, ss, 1, i:i + HD] for ss in range(subs) for i in range(0, part, HD)], axis=1
        )

    def finish(j):
        put(self_ref, j, run_out[j] * (1.0 / run_sum[j]))

    key_at = lax.broadcasted_iota(jnp.int32, (span, rows), 0)
    row_at = lax.broadcasted_iota(jnp.int32, (span, rows), 1) + s * rows
    bias = jnp.where(key_at <= row_at, 0.0, LOW)
    batch = 2 if heads % 2 == 0 else 1
    for first in range(0, heads, batch):
        js = range(first, first + batch)
        for cols in tiles:
            scs = [scores(j, keys_of(c, j), cols) + bias for j in js]
            tops = [jnp.max(sc, axis=0, keepdims=True) for sc in scs]
            ws = [jnp.exp2(sc - top) for sc, top in zip(scs, tops)]
            sums = [jnp.sum(w, axis=0, keepdims=True) for w in ws]
            outs = [
                jnp.dot(values_of(c, j), w.astype(jnp.bfloat16), preferred_element_type=jnp.float32)
                for j, w in zip(js, ws)
            ]
            for j, top, total, out in zip(js, tops, sums, outs):
                run_max[j, :, cols], run_sum[j, :, cols], run_out[j, :, cols] = top, total, out

    @pl.when(c == 0)
    def _():
        for j in range(heads):
            finish(j)

    @pl.loop(1, n)
    def _(d):
        cc = lax.rem(c + d, n)
        image_side(cc, s, 1).wait_recv()
        for e in range(1, subs):
            image_side(cc, s, e).start()

    @pl.loop(0, n)
    def _(cc):
        for e in range(1, subs):
            image_side(cc, lax.rem(s + e, subs), e).wait_recv()

    turns = c * heads // batch

    def place(x):
        return c - 1 - lax.div(x * batch, heads), lax.rem(x * batch, heads)

    def receive_head(b, j):
        up(b, j).wait_recv()

        @pl.when(c < n - 1)
        def _():
            up(b, j).start()

        for d in range(1, subs):
            side(b, j, s, d).start()

    def await_siblings(b, j):
        for d in range(1, subs):
            side(b, j, lax.rem(s + d, subs), d).wait_recv()

    def receive(x):
        b, first = place(x)
        for i in range(batch):
            receive_head(b, first + i)

    def consume(x):
        b, first = place(x)
        js = [first + i for i in range(batch)]
        for j in js:
            await_siblings(b, j)
        attend([(j, keys_of(b, j), values_of(b, j)) for j in js])

        @pl.when(b == 0)
        def _():
            for j in js:
                finish(j)

    @pl.when(turns > 1)
    def _():
        receive(jnp.int32(0))

    loads[5].wait()
    loads[6].wait()
    seen_images = tokens[pl.ds(mine, 1), :]
    visible = jnp.zeros_like(seen_images)
    for i in range(lengths.shape[0]):
        visible = visible + jnp.where(seen_images > i, lengths[i], 0)
    count = n * subs * image_rows
    allowed = lax.broadcasted_iota(jnp.int32, (count, rows), 0) < visible
    for j in range(heads):
        head = slice(j * HD, (j + 1) * HD)
        image_k = img[:, 0, :, head].reshape(count, HD)
        image_vt = img[:, 1, :, head].reshape(count, HD).T
        for g, cols in enumerate(tiles):
            sc = jnp.where(allowed, scores(j, image_k, cols), LOW)
            top = jnp.max(sc, axis=0, keepdims=True)
            w = jnp.where(allowed, jnp.exp2(sc - top), 0.0)
            total = jnp.sum(w, axis=0, keepdims=True)
            out = jnp.dot(image_vt, w.astype(jnp.bfloat16), preferred_element_type=jnp.float32)
            out = jnp.where(visible > 0, out * (1.0 / jnp.where(visible > 0, total, 1.0)), 0.0)
            at = (j * group + g) * HD
            cross_ref[:, at:at + HD] = out.astype(jnp.bfloat16).T

    def attend(items):
        for cols in tiles:
            js = [j for j, _, _ in items]
            olds = [run_max[j, :, cols] for j in js]
            totals = [run_sum[j, :, cols] for j in js]
            accs = [run_out[j, :, cols] for j in js]
            scs = [scores(j, key_rows, cols) for j, key_rows, _ in items]
            tops = [jnp.maximum(old, jnp.max(sc, axis=0, keepdims=True)) for old, sc in zip(olds, scs)]
            ws = [jnp.exp2(sc - top) for sc, top in zip(scs, tops)]
            factors = [jnp.exp2(old - top) for old, top in zip(olds, tops)]
            totals = [
                total * factor + jnp.sum(w, axis=0, keepdims=True)
                for total, factor, w in zip(totals, factors, ws)
            ]
            accs = [
                acc * factor + jnp.dot(vt, w.astype(jnp.bfloat16), preferred_element_type=jnp.float32)
                for acc, factor, (_, _, vt), w in zip(accs, factors, items, ws)
            ]
            for j, top, total, acc in zip(js, tops, totals, accs):
                run_max[j, :, cols], run_sum[j, :, cols], run_out[j, :, cols] = top, total, acc

    def attend_part(b, j, ss):
        cols = jnp.concatenate([kv[b, j, ss, 1, i:i + HD] for i in range(0, part, HD)], axis=1)
        attend([(j, kv[b, j, ss, 0], cols)])

    @pl.when(c > 0)
    def _():
        @pl.loop(1, turns - 1)
        def _(x):
            receive(x)
            consume(x - 1)

        @pl.when(turns > 1)
        def _():
            consume(turns - 2)

        b, first = place(turns - 1)
        for i in range(batch):
            receive_head(b, first + i)
            if i > 0:
                finish(first + i - 1)
            attend_part(b, first + i, s)
            await_siblings(b, first + i)
            for d in range(1, subs):
                attend_part(b, first + i, lax.rem(s + d, subs))
        finish(first + batch - 1)

    @pl.loop(1, n)
    def _(d):
        image_to(d).wait_send()

    @pl.loop(0, n)
    def _(cc):
        for d in range(1, subs):
            image_side(cc, s, d).wait_send()

    @pl.when(c < n - 1)
    def _():
        @pl.loop(0, c + 1)
        def _(b):
            for j in range(heads):
                up(b, j).wait_send()

    @pl.loop(0, c)
    def _(b):
        for j in range(heads):
            for d in range(1, subs):
                side(b, j, s, d).wait_send()


def local(queries, keys, values, image_keys, image_values, image_lengths, token_images):
    n, subs = lax.axis_size("ctx"), lax.axis_size("sub")
    rows, wide = queries.shape
    span, narrow = keys.shape
    heads, image_rows = narrow // HD, image_keys.shape[0]
    group = wide // narrow
    vmem = pl.BlockSpec(memory_space=pltpu.VMEM)
    hbm = pl.BlockSpec(memory_space=pltpu.HBM)
    dma = pltpu.SemaphoreType.DMA
    out = pltpu.VMEM((rows, wide), jnp.bfloat16)
    token_images = token_images.reshape(-1, rows)
    return pl.pallas_call(
        functools.partial(kernel, n, subs),
        out_shape=(out, out),
        in_specs=[hbm] * 7,
        out_specs=(vmem, vmem),
        scratch_shapes=[
            pltpu.SMEM(image_lengths.shape, jnp.int32),
            pltpu.VMEM(token_images.shape, jnp.int32),
            pltpu.VMEM((rows, wide), jnp.bfloat16),
            pltpu.VMEM((span, narrow), jnp.bfloat16),
            pltpu.VMEM((span, narrow), jnp.bfloat16),
            pltpu.VMEM((heads, HD, group * rows), jnp.bfloat16),
            pltpu.VMEM((n, heads, subs, 2, span // subs, HD), jnp.bfloat16),
            pltpu.VMEM((n * subs, 2, image_rows, narrow), jnp.bfloat16),
            pltpu.VMEM((heads, 1, group * rows), jnp.float32),
            pltpu.VMEM((heads, 1, group * rows), jnp.float32),
            pltpu.VMEM((heads, HD, group * rows), jnp.float32),
            dma((7,)),
            dma((n, heads, subs)),
            dma((n, heads)),
            dma((n, heads, subs - 1)),
            dma((n * subs,)),
            dma((n - 1,)),
            dma((n, subs - 1)),
        ],
        compiler_params=pltpu.CompilerParams(
            collective_id=0, has_side_effects=True, vmem_limit_bytes=60 * 1024 * 1024
        ),
    )(image_lengths, token_images, queries, keys, values, image_keys, image_values)


def solution(mesh):
    fine = P(("groups", "ctx", "sub"), "heads")
    block = P(("groups", "ctx"), "heads")
    in_specs = (fine, block, block, fine, fine, P("groups"), P("groups"))
    return jax.shard_map(local, mesh=mesh, in_specs=in_specs, out_specs=(fine, fine), check_vma=False)
```

```python
import functools
import math

import jax
import jax.numpy as jnp
from jax import lax
from jax.experimental import pallas as pl
from jax.experimental.pallas import tpu as pltpu
from jax.sharding import PartitionSpec as P

HD = 128
MESH = pl.DeviceIdType.MESH
LOW = -1e30
SCALE = math.log2(math.e) / math.sqrt(HD)


def kernel(
    n, subs, len_hbm, tok_hbm, q_hbm, k_hbm, v_hbm, ik_hbm, iv_hbm, self_ref, cross_ref,
    lengths, tokens, q, k, v, qt, kv, img, run_max, run_sum, run_out,
    in_sem, text_recv, up_send, side_send, img_recv, img_send, img_side,
):
    c, s = lax.axis_index("ctx"), lax.axis_index("sub")
    rows, span = q.shape[0], k.shape[0]
    heads = k.shape[1] // HD
    part = span // subs
    group = q.shape[1] // k.shape[1]
    image_rows = img.shape[2]
    mine = c * subs + s

    def sibling(d):
        return {"sub": lax.rem(s + d, subs)}

    barrier = pltpu.get_barrier_semaphore()

    @pl.loop(1, n)
    def _(d):
        pl.semaphore_signal(barrier, inc=1, device_id={"ctx": lax.rem(c + d, n)}, device_id_type=MESH)

    for d in range(1, subs):
        pl.semaphore_signal(barrier, inc=1, device_id=sibling(d), device_id_type=MESH)

    loads = [
        pltpu.make_async_copy(src, dst, in_sem.at[i])
        for i, (src, dst) in enumerate(
            [
                (k_hbm, k), (v_hbm, v), (ik_hbm, img.at[mine, 0]), (iv_hbm, img.at[mine, 1]),
                (q_hbm, q), (len_hbm, lengths), (tok_hbm, tokens),
            ]
        )
    ]
    for load in loads:
        load.start()

    def lay_out(ss):
        for j in range(heads):
            cols = slice(j * HD, (j + 1) * HD)
            kv[c, j, ss, 0] = k[pl.ds(ss * part, part), cols]
            for i in range(0, part, HD):
                kv[c, j, ss, 1, i:i + HD] = v[pl.ds(ss * part + i, HD), cols].T

    loads[0].wait()
    loads[1].wait()
    lay_out(s)
    pl.semaphore_wait(barrier, n - 1 + subs - 1)

    def up(b, j):
        return pltpu.make_async_remote_copy(
            kv.at[b, j, s], kv.at[b, j, s], up_send.at[b, j], text_recv.at[b, j, s],
            device_id={"ctx": lax.rem(c + 1, n)}, device_id_type=MESH,
        )

    def side(b, j, ss, d):
        return pltpu.make_async_remote_copy(
            kv.at[b, j, ss], kv.at[b, j, ss], side_send.at[b, j, d - 1], text_recv.at[b, j, ss],
            device_id=sibling(d), device_id_type=MESH,
        )

    def image_to(d):
        return pltpu.make_async_remote_copy(
            img.at[mine], img.at[mine], img_send.at[d - 1], img_recv.at[mine],
            device_id={"ctx": lax.rem(c + d, n)}, device_id_type=MESH,
        )

    def image_side(cc, ss, d):
        at = cc * subs + ss
        return pltpu.make_async_remote_copy(
            img.at[at], img.at[at], img_side.at[cc, d - 1], img_recv.at[at],
            device_id=sibling(d), device_id_type=MESH,
        )

    @pl.when(c < n - 1)
    def _():
        for j in range(heads):
            up(c, j).start()

    loads[2].wait()
    loads[3].wait()

    @pl.loop(1, n)
    def _(d):
        image_to(d).start()

    for d in range(1, subs):
        image_side(c, s, d).start()

    for d in range(1, subs):
        lay_out(lax.rem(s + d, subs))
    loads[4].wait()
    for j in range(heads):
        for g in range(group):
            h = j * group + g
            qt[j, :, g * rows:(g + 1) * rows] = q[:, h * HD:(h + 1) * HD].T

    def scores(j, key_rows):
        return jnp.dot(key_rows, qt[j], preferred_element_type=jnp.float32) * SCALE

    def wide(x):
        return jnp.concatenate([x] * group, axis=1)

    def put(ref, j, out):
        out = out.astype(jnp.bfloat16)
        for g in range(group):
            at = (j * group + g) * HD
            if not isinstance(at, int):
                at = pl.multiple_of(at, HD)
            ref[:, pl.ds(at, HD)] = out[:, g * rows:(g + 1) * rows].T

    def keys_of(b, j):
        return jnp.concatenate([kv[b, j, ss, 0] for ss in range(subs)], axis=0)

    def values_of(b, j):
        return jnp.concatenate(
            [kv[b, j, ss, 1, i:i + HD] for ss in range(subs) for i in range(0, part, HD)], axis=1
        )

    def finish(j):
        put(self_ref, j, run_out[j] * (1.0 / run_sum[j]))

    key_at = lax.broadcasted_iota(jnp.int32, (span, rows), 0)
    row_at = lax.broadcasted_iota(jnp.int32, (span, rows), 1) + s * rows
    bias = wide(jnp.where(key_at <= row_at, 0.0, LOW))
    batch = 2 if heads % 2 == 0 else 1
    for first in range(0, heads, batch):
        js = range(first, first + batch)
        scs = [scores(j, keys_of(c, j)) + bias for j in js]
        tops = [jnp.max(sc, axis=0, keepdims=True) for sc in scs]
        ws = [jnp.exp2(sc - top) for sc, top in zip(scs, tops)]
        sums = [jnp.sum(w, axis=0, keepdims=True) for w in ws]
        outs = [
            jnp.dot(values_of(c, j), w.astype(jnp.bfloat16), preferred_element_type=jnp.float32)
            for j, w in zip(js, ws)
        ]
        for j, top, total, out in zip(js, tops, sums, outs):
            run_max[j], run_sum[j], run_out[j] = top, total, out

    @pl.when(c == 0)
    def _():
        for j in range(heads):
            finish(j)

    @pl.loop(1, n)
    def _(d):
        cc = lax.rem(c + d, n)
        image_side(cc, s, 1).wait_recv()
        for e in range(1, subs):
            image_side(cc, s, e).start()

    @pl.loop(0, n)
    def _(cc):
        for e in range(1, subs):
            image_side(cc, lax.rem(s + e, subs), e).wait_recv()

    turns = c * heads // batch

    def place(x):
        return c - 1 - lax.div(x * batch, heads), lax.rem(x * batch, heads)

    def receive_head(b, j):
        up(b, j).wait_recv()

        @pl.when(c < n - 1)
        def _():
            up(b, j).start()

        for d in range(1, subs):
            side(b, j, s, d).start()

    def await_siblings(b, j):
        for d in range(1, subs):
            side(b, j, lax.rem(s + d, subs), d).wait_recv()

    def receive(x):
        b, first = place(x)
        for i in range(batch):
            receive_head(b, first + i)

    def consume(x):
        b, first = place(x)
        js = [first + i for i in range(batch)]
        for j in js:
            await_siblings(b, j)
        attend([(j, keys_of(b, j), values_of(b, j)) for j in js])

        @pl.when(b == 0)
        def _():
            for j in js:
                finish(j)

    @pl.when(turns > 1)
    def _():
        receive(jnp.int32(0))

    loads[5].wait()
    loads[6].wait()
    seen_images = tokens[pl.ds(mine, 1), :]
    visible = jnp.zeros_like(seen_images)
    for i in range(lengths.shape[0]):
        visible = visible + jnp.where(seen_images > i, lengths[i], 0)
    visible = wide(visible)
    count = n * subs * image_rows
    allowed = lax.broadcasted_iota(jnp.int32, (count, group * rows), 0) < visible
    for j in range(heads):
        cols = slice(j * HD, (j + 1) * HD)
        sc = jnp.where(allowed, scores(j, img[:, 0, :, cols].reshape(count, HD)), LOW)
        top = jnp.max(sc, axis=0, keepdims=True)
        w = jnp.where(allowed, jnp.exp2(sc - top), 0.0)
        total = jnp.sum(w, axis=0, keepdims=True)
        out = jnp.dot(
            img[:, 1, :, cols].reshape(count, HD).T, w.astype(jnp.bfloat16),
            preferred_element_type=jnp.float32,
        )
        out = jnp.where(visible > 0, out * (1.0 / jnp.where(visible > 0, total, 1.0)), 0.0)
        put(cross_ref, j, out)

    def attend(items):
        js = [j for j, _, _ in items]
        olds, totals, accs = [run_max[j] for j in js], [run_sum[j] for j in js], [run_out[j] for j in js]
        scs = [scores(j, key_rows) for j, key_rows, _ in items]
        tops = [jnp.maximum(old, jnp.max(sc, axis=0, keepdims=True)) for old, sc in zip(olds, scs)]
        ws = [jnp.exp2(sc - top) for sc, top in zip(scs, tops)]
        factors = [jnp.exp2(old - top) for old, top in zip(olds, tops)]
        totals = [
            total * factor + jnp.sum(w, axis=0, keepdims=True)
            for total, factor, w in zip(totals, factors, ws)
        ]
        accs = [
            acc * factor + jnp.dot(cols, w.astype(jnp.bfloat16), preferred_element_type=jnp.float32)
            for acc, factor, (_, _, cols), w in zip(accs, factors, items, ws)
        ]
        for j, top, total, acc in zip(js, tops, totals, accs):
            run_max[j], run_sum[j], run_out[j] = top, total, acc

    def attend_part(b, j, ss):
        cols = jnp.concatenate([kv[b, j, ss, 1, i:i + HD] for i in range(0, part, HD)], axis=1)
        attend([(j, kv[b, j, ss, 0], cols)])

    @pl.when(c > 0)
    def _():
        @pl.loop(1, turns - 1)
        def _(x):
            receive(x)
            consume(x - 1)

        @pl.when(turns > 1)
        def _():
            consume(turns - 2)

        b, first = place(turns - 1)
        for i in range(batch):
            receive_head(b, first + i)
            if i > 0:
                finish(first + i - 1)
            attend_part(b, first + i, s)
            await_siblings(b, first + i)
            for d in range(1, subs):
                attend_part(b, first + i, lax.rem(s + d, subs))
        finish(first + batch - 1)

    @pl.loop(1, n)
    def _(d):
        image_to(d).wait_send()

    @pl.loop(0, n)
    def _(cc):
        for d in range(1, subs):
            image_side(cc, s, d).wait_send()

    @pl.when(c < n - 1)
    def _():
        @pl.loop(0, c + 1)
        def _(b):
            for j in range(heads):
                up(b, j).wait_send()

    @pl.loop(0, c)
    def _(b):
        for j in range(heads):
            for d in range(1, subs):
                side(b, j, s, d).wait_send()


def local(queries, keys, values, image_keys, image_values, image_lengths, token_images):
    n, subs = lax.axis_size("ctx"), lax.axis_size("sub")
    rows, wide = queries.shape
    span, narrow = keys.shape
    heads, image_rows = narrow // HD, image_keys.shape[0]
    group = wide // narrow
    vmem = pl.BlockSpec(memory_space=pltpu.VMEM)
    hbm = pl.BlockSpec(memory_space=pltpu.HBM)
    dma = pltpu.SemaphoreType.DMA
    out = pltpu.VMEM((rows, wide), jnp.bfloat16)
    token_images = token_images.reshape(-1, rows)
    return pl.pallas_call(
        functools.partial(kernel, n, subs),
        out_shape=(out, out),
        in_specs=[hbm] * 7,
        out_specs=(vmem, vmem),
        scratch_shapes=[
            pltpu.SMEM(image_lengths.shape, jnp.int32),
            pltpu.VMEM(token_images.shape, jnp.int32),
            pltpu.VMEM((rows, wide), jnp.bfloat16),
            pltpu.VMEM((span, narrow), jnp.bfloat16),
            pltpu.VMEM((span, narrow), jnp.bfloat16),
            pltpu.VMEM((heads, HD, group * rows), jnp.bfloat16),
            pltpu.VMEM((n, heads, subs, 2, span // subs, HD), jnp.bfloat16),
            pltpu.VMEM((n * subs, 2, image_rows, narrow), jnp.bfloat16),
            pltpu.VMEM((heads, 1, group * rows), jnp.float32),
            pltpu.VMEM((heads, 1, group * rows), jnp.float32),
            pltpu.VMEM((heads, HD, group * rows), jnp.float32),
            dma((7,)),
            dma((n, heads, subs)),
            dma((n, heads)),
            dma((n, heads, subs - 1)),
            dma((n * subs,)),
            dma((n - 1,)),
            dma((n, subs - 1)),
        ],
        compiler_params=pltpu.CompilerParams(
            collective_id=0, has_side_effects=True, vmem_limit_bytes=60 * 1024 * 1024
        ),
    )(image_lengths, token_images, queries, keys, values, image_keys, image_values)


def solution(mesh):
    fine = P(("groups", "ctx", "sub"), "heads")
    block = P(("groups", "ctx"), "heads")
    in_specs = (fine, block, block, fine, fine, P("groups"), P("groups"))
    return jax.shard_map(local, mesh=mesh, in_specs=in_specs, out_specs=(fine, fine), check_vma=False)
```
